32 devices in a mesh: box: 32 (over z, y, x, core).
Axes of the slice: x: 2, y: 2, z: 4, core: 2. Of those that a mesh axis runs over, the one named last changes fastest.
Arguments:
- fine_mult: bfloat16 [32768, 128], P('box'), may hold values from -6 to 6
- parent_mult: bfloat16 [4096, 128], P('box'), may hold values from -6 to 6
- fine_mask: int32 [20, 32768], P(None, 'box'), may hold values from 0 to 65535, as said below
- parent_mask: int32 [20, 4096], P(None, 'box'), may hold values from 0 to 65535, as said below
- kernels: bfloat16 [316, 128, 128], replicated, may hold values from -0.0390625 to 0.0390625
- shift_ops: bfloat16 [8, 128, 128], replicated, may hold values from -0.5 to 0.5
Outputs:
- fine_local: bfloat16 [32768, 128], P('box')
- parent_local: bfloat16 [4096, 128], P('box')
The draws below stay inside these ranges and needn't reach their ends.
Inputs may be any that keep to these rules, and one draw needn't show every extreme that they name: `fine_mask`: bit d mod 16 of word floor(d / 16) of box t is set only where the box at t's coordinates plus offset d lies inside the grid and its parent is one of the 27 boxes around t's parent; bits 12 to 15 of word 19 are zero; sources in many regions are missing from the lists. `parent_mask`: the same rule at the parent level.
All inputs are finite; a program needn't handle non-finite values.
Results may differ from the reference program's by a relative error of at most 0.0027.
Values may be sent and summed in bfloat16 or wider, within the bound.
A program may use at most 320 MiB of HBM per device.

```python
import jax
import jax.numpy as jnp
import numpy as np
from jax import lax

R = 128
DIRS = 316
BOXES = 32768
PBOXES = 4096


def direction_table_drawn():
    listing = []
    for group_first in range(3):
        for group_second in range(3):
            for group_third in range(3):
                ranges_all = []
                for marker in (group_first, group_second, group_third):
                    if marker == 0:
                        ranges_all.append([-2, -1, 0, 1, 2])
                    elif marker == 1:
                        ranges_all.append([-3])
                    else:
                        ranges_all.append([3])
                for along_one in ranges_all[0]:
                    for along_two in ranges_all[1]:
                        for along_three in ranges_all[2]:
                            if max(abs(along_one), abs(along_two), abs(along_three)) >= 2:
                                listing.append((along_one, along_two, along_three, group_first, group_second, group_third))
    return np.array(listing, np.int32)


def packed_lists(key, box_count):
    total_bits = box_count.bit_length() - 1
    positions = jnp.arange(box_count, dtype=jnp.int32)
    coords = [jnp.zeros((box_count,), jnp.int32) for dim_code in range(3)]
    domain = [1, 1, 1]
    for position in range(total_bits):
        dim_code = 2 - position % 3
        coords[dim_code] = coords[dim_code] + jnp.left_shift(jnp.right_shift(positions, position) & 1, position // 3)
        domain[dim_code] = domain[dim_code] * 2
    region_bits = min(6, total_bits)
    regions = jnp.right_shift(positions, total_bits - region_bits)
    region_levels = jax.random.randint(jax.random.fold_in(key, 1), (2 ** region_bits,), 1, 5)
    occupied = jax.random.randint(jax.random.fold_in(key, 2), (box_count,), 0, 4) < region_levels[regions]
    offsets_table = direction_table_drawn()
    packed = [jnp.zeros((box_count,), jnp.int32) for word_number in range(20)]
    for number in range(offsets_table.shape[0]):
        inside_all = jnp.ones((box_count,), bool)
        near_all = jnp.ones((box_count,), bool)
        shifted = []
        for dim_code in range(3):
            moved = coords[dim_code] + int(offsets_table[number, dim_code])
            inside_all = inside_all & (moved >= 0) & (moved < domain[dim_code])
            parent_gap = jnp.right_shift(moved, 1) - jnp.right_shift(coords[dim_code], 1)
            near_all = near_all & (parent_gap >= -1) & (parent_gap <= 1)
            shifted.append(moved)
        source_index = jnp.zeros((box_count,), jnp.int32)
        for position in range(total_bits):
            dim_code = 2 - position % 3
            source_index = source_index + jnp.left_shift(jnp.right_shift(shifted[dim_code], position // 3) & 1, position)
        source_index = jnp.where(inside_all, source_index, 0)
        bit_value = (inside_all & near_all & occupied[source_index]).astype(jnp.int32)
        packed[number // 16] = packed[number // 16] + jnp.left_shift(bit_value, number % 16)
    return jnp.stack(packed)


def draw_fine_mask(key, part):
    return packed_lists(jax.random.fold_in(key, 11), BOXES)


def draw_parent_mask(key, part):
    return packed_lists(jax.random.fold_in(key, 12), PBOXES)


def block_scale(key, dims, shards, low, top_value):
    gain, own = 1.0, jax.random.fold_in(key, 6)
    for axis_at, shards_of in shards:
        draws = jnp.exp(jax.random.uniform(jax.random.fold_in(own, axis_at), (shards_of,), jnp.float32, low / len(shards), top_value / len(shards)))
        gain = gain * jnp.repeat(draws, dims[axis_at] // shards_of).reshape([-1 if axis == axis_at else 1 for axis in range(len(dims))])
    return gain


def bell_draw(stream_key, shape, width, most, split=(), held_as=jnp.bfloat16):
    values = width * jax.random.normal(stream_key, shape, jnp.float32)
    if split:
        values = values * block_scale(stream_key, shape, split, -0.22, 0.18)
    return jnp.clip(values, -most, most).astype(held_as)


def setup_inputs(seed: int = 0) -> dict:
    arg_keys = jax.random.split(jax.random.key(seed), 7)
    return {
        "fine_mult": bell_draw(arg_keys[0], (BOXES, R), 1.0, 6.0, ((0, 32),)),
        "parent_mult": bell_draw(arg_keys[1], (PBOXES, R), 1.0, 6.0, ((0, 32),)),
        "fine_mask": draw_fine_mask(jax.random.fold_in(arg_keys[6], 71), 0),
        "parent_mask": draw_parent_mask(jax.random.fold_in(arg_keys[6], 71), 0),
        "kernels": bell_draw(arg_keys[4], (DIRS, R, R), (R * 189) ** -0.5, 0.0390625),
        "shift_ops": bell_draw(arg_keys[5], (8, R, R), R ** -0.5, 0.5),
    }


def direction_table():
    listing = []
    for group_first in range(3):
        for group_second in range(3):
            for group_third in range(3):
                ranges_all = []
                for marker in (group_first, group_second, group_third):
                    if marker == 0:
                        ranges_all.append([-2, -1, 0, 1, 2])
                    elif marker == 1:
                        ranges_all.append([-3])
                    else:
                        ranges_all.append([3])
                for along_one in ranges_all[0]:
                    for along_two in ranges_all[1]:
                        for along_three in ranges_all[2]:
                            if max(abs(along_one), abs(along_two), abs(along_three)) >= 2:
                                listing.append((along_one, along_two, along_three, group_first, group_second, group_third))
    return np.array(listing, np.int32)


def grid_order(total_bits):
    axes_order = []
    extents = []
    for target in range(3):
        chosen = [position for position in range(total_bits - 1, -1, -1) if 2 - position % 3 == target]
        axes_order += [total_bits - 1 - position for position in chosen]
        extents.append(2 ** len(chosen))
    return axes_order, extents


def to_grid(morton_rows, total_bits):
    axes_order, extents = grid_order(total_bits)
    trailing = morton_rows.shape[1:]
    bitwise = morton_rows.reshape((2,) * total_bits + trailing)
    permuted = jnp.transpose(bitwise, tuple(axes_order) + tuple(range(total_bits, total_bits + len(trailing))))
    return permuted.reshape(tuple(extents) + trailing)


def from_grid(gridded, total_bits):
    axes_order, extents = grid_order(total_bits)
    trailing = gridded.shape[3:]
    bitwise = gridded.reshape((2,) * total_bits + trailing)
    inverse = [0] * total_bits
    for position, source in enumerate(axes_order):
        inverse[source] = position
    permuted = jnp.transpose(bitwise, tuple(inverse) + tuple(range(total_bits, total_bits + len(trailing))))
    return permuted.reshape((2 ** total_bits,) + trailing)


def level_sum(mult, packed, kernels, factor):
    level_bits = mult.shape[0].bit_length() - 1
    rank_width = mult.shape[1]
    gridded = to_grid(mult, level_bits)
    padded = jnp.pad(gridded, ((3, 3), (3, 3), (3, 3), (0, 0)))
    word_grid = to_grid(jnp.transpose(packed), level_bits)
    offsets_table = jnp.asarray(direction_table()[:, :3])
    numbers = jnp.arange(kernels.shape[0], dtype=jnp.int32)
    extents = tuple(gridded.shape[:3])
    zero_index = jnp.zeros((), jnp.int32)

    def one_direction(accumulated, inputs):
        kernel, offset, number = inputs
        starts = (3 + offset[0], 3 + offset[1], 3 + offset[2], zero_index)
        window = lax.dynamic_slice(padded, starts, extents + (rank_width,))
        word_slice = lax.dynamic_index_in_dim(word_grid, number // 16, axis=3, keepdims=False)
        present = (jnp.right_shift(word_slice, number % 16) & 1).astype(jnp.bfloat16)
        masked = (window * present[..., None]).reshape(-1, rank_width)
        product = jnp.dot(masked.astype(jnp.float32), kernel.astype(jnp.float32), preferred_element_type=jnp.float32)
        return accumulated + product.reshape(accumulated.shape), None

    start_value = jnp.zeros(extents + (rank_width,), jnp.float32)
    accumulated, unused = lax.scan(one_direction, start_value, (kernels, offsets_table, numbers))
    return from_grid(accumulated * factor, level_bits)


def reference(fine_mult, parent_mult, fine_mask, parent_mask, kernels, shift_ops):
    parent_local = level_sum(parent_mult, parent_mask, kernels, 0.5).astype(jnp.bfloat16)
    rank_width = fine_mult.shape[1]
    translated = jnp.einsum("pr,krs->pks", parent_local.astype(jnp.float32), shift_ops.astype(jnp.float32))
    translated = translated.reshape(fine_mult.shape[0], rank_width)
    fine_total = level_sum(fine_mult, fine_mask, kernels, 1.0) + translated
    return (fine_total.astype(jnp.bfloat16), parent_local)
```

```python
import functools

import jax
import jax.numpy as jnp
import numpy as np
from jax import lax
from jax.experimental import pallas as pl
from jax.experimental.pallas import tpu as pltpu
from jax.sharding import PartitionSpec as P

CHUNK = 9


def direction_table():
    listing = []
    for g1 in range(3):
        for g2 in range(3):
            for g3 in range(3):
                spans = [([-2, -1, 0, 1, 2], [-3], [3])[g] for g in (g1, g2, g3)]
                for o1 in spans[0]:
                    for o2 in spans[1]:
                        for o3 in spans[2]:
                            if max(abs(o1), abs(o2), abs(o3)) >= 2:
                                listing.append((o1, o2, o3))
    return listing


def class_tables():
    dirs, wins = [], []
    for c in range(8):
        child = (c >> 2 & 1, c >> 1 & 1, c & 1)
        count = 0
        for number, offset in enumerate(direction_table()):
            moved = [child[k] + offset[k] for k in range(3)]
            shift = [m >> 1 for m in moved]
            if max(abs(s) for s in shift) > 1:
                continue
            source = (moved[0] & 1) * 4 + (moved[1] & 1) * 2 + (moved[2] & 1)
            delta = (shift[0] + 1) * 9 + (shift[1] + 1) * 3 + shift[2] + 1
            dirs.append(number)
            wins.append(delta * 8 + source)
            count += 1
        assert count == 189
    return np.array(dirs, np.int32), np.array(wins, np.int32)


def grid_order(total_bits):
    order, extents = [], []
    for target in range(3):
        chosen = [k for k in range(total_bits - 1, -1, -1) if 2 - k % 3 == target]
        order += [total_bits - 1 - k for k in chosen]
        extents.append(2 ** len(chosen))
    return order, extents


def to_grid(rows, total_bits):
    order, extents = grid_order(total_bits)
    trailing = rows.shape[1:]
    bitwise = rows.reshape((2,) * total_bits + trailing)
    kept = tuple(range(total_bits, total_bits + len(trailing)))
    return jnp.transpose(bitwise, tuple(order) + kept).reshape(tuple(extents) + trailing)


def grid_index(morton, extents):
    coords = [0, 0, 0]
    for k in range(morton.bit_length()):
        coords[2 - k % 3] |= (morton >> k & 1) << (k // 3)
    return (coords[0] * extents[1] + coords[1]) * extents[2] + coords[2]


def shift_route(count, level_bits, dim, step):
    bits = count.bit_length() - 1
    owned = [k for k in range(bits) if 2 - (level_bits + k) % 3 == dim]
    route = []
    for src in range(count):
        at = sum((src >> k & 1) << n for n, k in enumerate(owned)) + step
        if 0 <= at < 2 ** len(owned):
            dst = src
            for n, k in enumerate(owned):
                dst = dst & ~(1 << k) | (at >> n & 1) << k
            route.append((src, dst))
    return route


def extend(blocks, level_bits, count):
    for dim in range(3):
        halos = []
        for step in (1, -1):
            faces = []
            for block in blocks:
                size = block.shape[dim]
                start = size - 1 if step == 1 else 0
                faces.append(lax.slice_in_dim(block, start, start + 1, axis=dim))
            flat = jnp.concatenate([f.reshape((-1,) + f.shape[3:]) for f in faces])
            got = lax.ppermute(flat, "box", shift_route(count, level_bits, dim, step))
            parts, row = [], 0
            for f in faces:
                rows = f.shape[0] * f.shape[1] * f.shape[2]
                parts.append(got[row : row + rows].reshape(f.shape))
                row += rows
            halos.append(parts)
        blocks = [
            jnp.concatenate([low, block, high], axis=dim)
            for low, block, high in zip(halos[0], blocks, halos[1])
        ]
    return blocks


def interact_kernel(
    fext, gext, dtab, wtab, ext_f, ext_p, words, bits, shift, kernels,
    fine_out, parent_out, kv, win, wb, acc_f, acc_p, par, sem,
):
    nf, ng = fext[0] * fext[1] * fext[2], gext[0] * gext[1] * gext[2]
    rows = nf + ng
    tiles = rows // 16
    fetch = pltpu.make_async_copy(kernels, kv, sem)
    fetch.start()

    def build(index, carry):
        delta, source = index // 8, index % 8
        dx, dy, dz = delta // 9, delta // 3 % 3, delta % 3
        for ref, ext, base in ((ext_f, fext, 0), (ext_p, gext, nf)):
            got = []
            for x in range(ext[0]):
                for y in range(ext[1]):
                    first = ((x + dx) * (ext[1] + 2) + y + dy) * (ext[2] + 2) + dz
                    got.append(ref[pl.ds(first * 8 + source, ext[2], stride=8), :])
            stack = jnp.concatenate(got, axis=0).astype(jnp.bfloat16)
            count = stack.shape[0] // 16
            win[index, pl.ds(base // 16, count)] = stack.reshape(count, 16, 128)
        return carry

    lax.fori_loop(0, 216, build, 0)
    fetch.wait()

    def one_class(c, carry):
        mine = words[c]
        for w in range(20):
            spread = jnp.broadcast_to(mine[:, w : w + 1], (rows, 128)).astype(jnp.int16)
            wb[w] = spread.reshape(tiles, 16, 128)

        def step(j, acc):
            lhs, rhs = [], []
            for i in range(CHUNK):
                n = c * 189 + j * CHUNK + i
                d = dtab[n]
                hit = (wb[d // 16] & bits[d % 16][None]) != 0
                x = win[wtab[n]]
                lhs.append(jnp.where(hit, x, jnp.zeros_like(x)).reshape(rows, 128))
                rhs.append(kv[d])
            return acc + jnp.dot(
                jnp.concatenate(lhs, axis=1),
                jnp.concatenate(rhs, axis=0),
                preferred_element_type=jnp.float32,
            )

        acc = lax.fori_loop(0, 189 // CHUNK, step, jnp.zeros((rows, 128), jnp.float32))
        acc_f[pl.ds(pl.multiple_of(c * nf, 16), nf), :] = acc[:nf]
        acc_p[pl.ds(pl.multiple_of(c * ng, 16), ng), :] = (
            (acc[nf:] * 0.5).astype(jnp.bfloat16).astype(jnp.float32)
        )
        return carry

    lax.fori_loop(0, 8, one_class, 0)

    for c in range(8):
        cx, cy, cz = c >> 2 & 1, c >> 1 & 1, c & 1
        for gx in range(gext[0]):
            for gy in range(gext[1]):
                first = c * ng + (gx * gext[1] + gy) * gext[2]
                to = ((2 * gx + cx) * fext[1] + 2 * gy + cy) * fext[2] + cz
                par[pl.ds(to, gext[2], stride=2), :] = acc_p[pl.ds(first, gext[2]), :]
    local = par[...].astype(jnp.bfloat16)
    for c in range(8):
        acc_f[pl.ds(c * nf, nf), :] += jnp.dot(
            local, shift[c], preferred_element_type=jnp.float32
        )
    for ref, out, ext, total in ((acc_f, fine_out, fext, nf), (acc_p, parent_out, gext, ng)):
        for m in range(0, total, 2):
            pair = [
                ref[pl.ds(grid_index(m + k, ext), 8, stride=total), :] for k in range(2)
            ]
            out[pl.ds(m * 8, 16), :] = jnp.concatenate(pair, axis=0).astype(jnp.bfloat16)


def on_device(fine_mult, parent_mult, fine_mask, parent_mask, kernels, shift_ops):
    count = lax.axis_size("box")
    width = fine_mult.shape[1]
    fbits = fine_mult.shape[0].bit_length() - 4
    pbits = parent_mult.shape[0].bit_length() - 4
    fext, gext = tuple(grid_order(fbits)[1]), tuple(grid_order(pbits)[1])
    nf, ng = 2**fbits, 2**pbits
    rows = nf + ng

    blocks = [
        to_grid(fine_mult.reshape(nf, 8, width), fbits),
        to_grid(parent_mult.reshape(ng, 8, width), pbits),
    ]
    ext_f, ext_p = (
        b.reshape(-1, width).astype(jnp.float32) for b in extend(blocks, fbits + 3, count)
    )

    def by_class(mask, bits, total):
        grid = to_grid(jnp.transpose(mask).reshape(total, 8, 20), bits)
        return jnp.transpose(grid.reshape(total, 8, 20), (1, 0, 2))

    words = jnp.concatenate(
        [by_class(fine_mask, fbits, nf), by_class(parent_mask, pbits, ng)], axis=1
    )
    dtab, wtab = class_tables()
    flags = np.array([1 << k if k < 15 else -(1 << 15) for k in range(16)], np.int16)
    bits = np.broadcast_to(flags[:, None, None], (16, 16, 128))
    smem = pl.BlockSpec(memory_space=pltpu.SMEM)
    vmem = pl.BlockSpec(memory_space=pltpu.VMEM)
    return pl.pallas_call(
        functools.partial(interact_kernel, fext, gext),
        out_shape=[
            jax.ShapeDtypeStruct(fine_mult.shape, jnp.bfloat16),
            jax.ShapeDtypeStruct(parent_mult.shape, jnp.bfloat16),
        ],
        in_specs=[smem, smem, vmem, vmem, vmem, vmem, vmem, pl.BlockSpec(memory_space=pl.ANY)],
        out_specs=[vmem, vmem],
        scratch_shapes=[
            pltpu.VMEM(kernels.shape, jnp.bfloat16),
            pltpu.VMEM((216, rows // 16, 16, width), jnp.bfloat16),
            pltpu.VMEM((20, rows // 16, 16, width), jnp.int16),
            pltpu.VMEM((8 * nf, width), jnp.float32),
            pltpu.VMEM((8 * ng, width), jnp.float32),
            pltpu.VMEM((nf, width), jnp.float32),
            pltpu.SemaphoreType.DMA,
        ],
        compiler_params=pltpu.CompilerParams(vmem_limit_bytes=56 * 1024 * 1024),
        cost_estimate=pl.CostEstimate(
            flops=2 * 8 * rows * 189 * width * width,
            bytes_accessed=kernels.size * 2,
            transcendentals=0,
        ),
        name="interact",
    )(dtab, wtab, ext_f, ext_p, words, jnp.asarray(bits), shift_ops, kernels)


def solution(mesh):
    return jax.shard_map(
        on_device,
        mesh=mesh,
        in_specs=(P("box", None), P("box", None), P(None, "box"), P(None, "box"), P(), P()),
        out_specs=(P("box", None), P("box", None)),
        check_vma=False,
    )
```

```python
import functools

import jax
import jax.numpy as jnp
import numpy as np
from jax import lax
from jax.experimental import pallas as pl
from jax.experimental.pallas import tpu as pltpu
from jax.sharding import PartitionSpec as P

CHUNK = 14


def direction_table():
    listing = []
    for g1 in range(3):
        for g2 in range(3):
            for g3 in range(3):
                spans = [([-2, -1, 0, 1, 2], [-3], [3])[g] for g in (g1, g2, g3)]
                for o1 in spans[0]:
                    for o2 in spans[1]:
                        for o3 in spans[2]:
                            if max(abs(o1), abs(o2), abs(o3)) >= 2:
                                listing.append((o1, o2, o3))
    return listing


def window_table():
    table = np.zeros((8, 316), np.int32)
    for c in range(8):
        child = (c >> 2 & 1, c >> 1 & 1, c & 1)
        for number, offset in enumerate(direction_table()):
            moved = [child[k] + offset[k] for k in range(3)]
            shift = [m >> 1 for m in moved]
            if max(abs(s) for s in shift) <= 1:
                source = (moved[0] & 1) * 4 + (moved[1] & 1) * 2 + (moved[2] & 1)
                delta = (shift[0] + 1) * 9 + (shift[1] + 1) * 3 + shift[2] + 1
                table[c, number] = delta * 8 + source
    return table.reshape(-1)


def groups():
    runs = []
    for number, offset in enumerate(direction_table()):
        classes = tuple(
            c for c in range(8)
            if all(
                abs(offset[k]) < 3 or (c >> (2 - k) & 1) == (offset[k] < 0) for k in range(3)
            )
        )
        if runs and runs[-1][2] == classes:
            runs[-1][1] += 1
        else:
            runs.append([number, 1, classes])
    return runs


def grid_order(total_bits):
    order, extents = [], []
    for target in range(3):
        chosen = [k for k in range(total_bits - 1, -1, -1) if 2 - k % 3 == target]
        order += [total_bits - 1 - k for k in chosen]
        extents.append(2 ** len(chosen))
    return order, extents


def to_grid(rows, total_bits):
    order, extents = grid_order(total_bits)
    trailing = rows.shape[1:]
    bitwise = rows.reshape((2,) * total_bits + trailing)
    kept = tuple(range(total_bits, total_bits + len(trailing)))
    return jnp.transpose(bitwise, tuple(order) + kept).reshape(tuple(extents) + trailing)


def grid_index(morton, extents):
    coords = [0, 0, 0]
    for k in range(morton.bit_length()):
        coords[2 - k % 3] |= (morton >> k & 1) << (k // 3)
    return (coords[0] * extents[1] + coords[1]) * extents[2] + coords[2]


def shift_route(count, level_bits, dim, step):
    bits = count.bit_length() - 1
    owned = [k for k in range(bits) if 2 - (level_bits + k) % 3 == dim]
    route = []
    for src in range(count):
        at = sum((src >> k & 1) << n for n, k in enumerate(owned)) + step
        if 0 <= at < 2 ** len(owned):
            dst = src
            for n, k in enumerate(owned):
                dst = dst & ~(1 << k) | (at >> n & 1) << k
            route.append((src, dst))
    return route


def extend(blocks, level_bits, count):
    for dim in range(3):
        halos = []
        for step in (1, -1):
            faces = []
            for block in blocks:
                size = block.shape[dim]
                start = size - 1 if step == 1 else 0
                faces.append(lax.slice_in_dim(block, start, start + 1, axis=dim))
            flat = jnp.concatenate([f.reshape((-1,) + f.shape[3:]) for f in faces])
            got = lax.ppermute(flat, "box", shift_route(count, level_bits, dim, step))
            parts, row = [], 0
            for f in faces:
                rows = f.shape[0] * f.shape[1] * f.shape[2]
                parts.append(got[row : row + rows].reshape(f.shape))
                row += rows
            halos.append(parts)
        blocks = [
            jnp.concatenate([low, block, high], axis=dim)
            for low, block, high in zip(halos[0], blocks, halos[1])
        ]
    return blocks


def interact_kernel(
    fext, gext, wtab, ext_f, ext_p, words, bits, shift, kernels,
    fine_out, parent_out, kv, win, wb, acc, acc_f, acc_p, par, sem,
):
    nf, ng = fext[0] * fext[1] * fext[2], gext[0] * gext[1] * gext[2]
    rows = nf + ng
    tiles = rows // 16
    fetch = pltpu.make_async_copy(kernels, kv, sem)
    fetch.start()

    def build(index, carry):
        delta, source = index // 8, index % 8
        dx, dy, dz = delta // 9, delta // 3 % 3, delta % 3
        for ref, ext, base in ((ext_f, fext, 0), (ext_p, gext, nf)):
            got = []
            for x in range(ext[0]):
                for y in range(ext[1]):
                    first = ((x + dx) * (ext[1] + 2) + y + dy) * (ext[2] + 2) + dz
                    got.append(ref[pl.ds(first * 8 + source, ext[2], stride=8), :])
            stack = jnp.concatenate(got, axis=0).astype(jnp.bfloat16)
            count = stack.shape[0] // 16
            win[index, pl.ds(base // 16, count)] = stack.reshape(count, 16, 128)
        return carry

    lax.fori_loop(0, 216, build, 0)
    fetch.wait()

    def spread(c, carry):
        mine = words[c]
        for w in range(20):
            wide = jnp.broadcast_to(mine[:, w : w + 1], (rows, 128)).astype(jnp.int16)
            wb[c, w] = wide.reshape(tiles, 16, 128)
        acc[c] = jnp.zeros((rows, 128), jnp.float32)
        return carry

    lax.fori_loop(0, 8, spread, 0)

    def contract(start, count, classes):
        lhs = []
        for c in classes:
            line = []
            for i in range(count):
                d = start + i
                hit = (wb[c, d // 16] & bits[d % 16][None]) != 0
                x = win[wtab[c * 316 + d]]
                line.append(jnp.where(hit, x, jnp.zeros_like(x)).reshape(rows, 128))
            lhs.append(jnp.concatenate(line, axis=1))
        total = jnp.dot(
            jnp.concatenate(lhs, axis=0),
            kv[pl.ds(start, count)].reshape(count * 128, 128),
            preferred_element_type=jnp.float32,
        )
        for k, c in enumerate(classes):
            acc[c] += total[k * rows : (k + 1) * rows]

    for start, count, classes in groups():
        if count > CHUNK and len(classes) == 8:
            def step(j, carry, start=start, classes=classes):
                contract(start + j * CHUNK, CHUNK, classes)
                return carry

            lax.fori_loop(0, count // CHUNK, step, 0)
        else:
            contract(start, count, classes)

    for c in range(8):
        acc_f[pl.ds(c * nf, nf), :] = acc[c, :nf]
        acc_p[pl.ds(c * ng, ng), :] = (
            (acc[c, nf:] * 0.5).astype(jnp.bfloat16).astype(jnp.float32)
        )
    for c in range(8):
        cx, cy, cz = c >> 2 & 1, c >> 1 & 1, c & 1
        for gx in range(gext[0]):
            for gy in range(gext[1]):
                first = c * ng + (gx * gext[1] + gy) * gext[2]
                to = ((2 * gx + cx) * fext[1] + 2 * gy + cy) * fext[2] + cz
                par[pl.ds(to, gext[2], stride=2), :] = acc_p[pl.ds(first, gext[2]), :]
    local = par[...].astype(jnp.bfloat16)
    for c in range(8):
        acc_f[pl.ds(c * nf, nf), :] += jnp.dot(
            local, shift[c], preferred_element_type=jnp.float32
        )
    for ref, out, ext, total in ((acc_f, fine_out, fext, nf), (acc_p, parent_out, gext, ng)):
        for m in range(0, total, 2):
            pair = [
                ref[pl.ds(grid_index(m + k, ext), 8, stride=total), :] for k in range(2)
            ]
            out[pl.ds(m * 8, 16), :] = jnp.concatenate(pair, axis=0).astype(jnp.bfloat16)


def on_device(fine_mult, parent_mult, fine_mask, parent_mask, kernels, shift_ops):
    count = lax.axis_size("box")
    width = fine_mult.shape[1]
    fbits = fine_mult.shape[0].bit_length() - 4
    pbits = parent_mult.shape[0].bit_length() - 4
    fext, gext = tuple(grid_order(fbits)[1]), tuple(grid_order(pbits)[1])
    nf, ng = 2**fbits, 2**pbits
    rows = nf + ng

    blocks = [
        to_grid(fine_mult.reshape(nf, 8, width), fbits),
        to_grid(parent_mult.reshape(ng, 8, width), pbits),
    ]
    ext_f, ext_p = (
        b.reshape(-1, width).astype(jnp.float32) for b in extend(blocks, fbits + 3, count)
    )

    def by_class(mask, bits, total):
        grid = to_grid(jnp.transpose(mask).reshape(total, 8, 20), bits)
        return jnp.transpose(grid.reshape(total, 8, 20), (1, 0, 2))

    words = jnp.concatenate(
        [by_class(fine_mask, fbits, nf), by_class(parent_mask, pbits, ng)], axis=1
    )
    wtab = window_table()
    flags = np.array([1 << k if k < 15 else -(1 << 15) for k in range(16)], np.int16)
    bits = np.broadcast_to(flags[:, None, None], (16, 16, 128))
    smem = pl.BlockSpec(memory_space=pltpu.SMEM)
    vmem = pl.BlockSpec(memory_space=pltpu.VMEM)
    return pl.pallas_call(
        functools.partial(interact_kernel, fext, gext),
        out_shape=[
            jax.ShapeDtypeStruct(fine_mult.shape, jnp.bfloat16),
            jax.ShapeDtypeStruct(parent_mult.shape, jnp.bfloat16),
        ],
        in_specs=[smem, vmem, vmem, vmem, vmem, vmem, pl.BlockSpec(memory_space=pl.ANY)],
        out_specs=[vmem, vmem],
        scratch_shapes=[
            pltpu.VMEM(kernels.shape, jnp.bfloat16),
            pltpu.VMEM((216, rows // 16, 16, width), jnp.bfloat16),
            pltpu.VMEM((8, 20, rows // 16, 16, width), jnp.int16),
            pltpu.VMEM((8, rows, width), jnp.float32),
            pltpu.VMEM((8 * nf, width), jnp.float32),
            pltpu.VMEM((8 * ng, width), jnp.float32),
            pltpu.VMEM((nf, width), jnp.float32),
            pltpu.SemaphoreType.DMA,
        ],
        compiler_params=pltpu.CompilerParams(vmem_limit_bytes=56 * 1024 * 1024),
        cost_estimate=pl.CostEstimate(
            flops=2 * 8 * rows * 189 * width * width,
            bytes_accessed=kernels.size * 2,
            transcendentals=0,
        ),
        name="interact",
    )(wtab, ext_f, ext_p, words, jnp.asarray(bits), shift_ops, kernels)


def solution(mesh):
    return jax.shard_map(
        on_device,
        mesh=mesh,
        in_specs=(P("box", None), P("box", None), P(None, "box"), P(None, "box"), P(), P()),
        out_specs=(P("box", None), P("box", None)),
        check_vma=False,
    )
```

```python
import functools

import jax
import jax.numpy as jnp
import numpy as np
from jax import lax
from jax.experimental import pallas as pl
from jax.experimental.pallas import tpu as pltpu
from jax.sharding import PartitionSpec as P

CHUNK = 14


def direction_table():
    listing = []
    for g1 in range(3):
        for g2 in range(3):
            for g3 in range(3):
                spans = [([-2, -1, 0, 1, 2], [-3], [3])[g] for g in (g1, g2, g3)]
                for o1 in spans[0]:
                    for o2 in spans[1]:
                        for o3 in spans[2]:
                            if max(abs(o1), abs(o2), abs(o3)) >= 2:
                                listing.append((o1, o2, o3))
    return listing


def window_table():
    table = np.zeros((8, 316), np.int32)
    for c in range(8):
        child = (c >> 2 & 1, c >> 1 & 1, c & 1)
        for number, offset in enumerate(direction_table()):
            moved = [child[k] + offset[k] for k in range(3)]
            shift = [m >> 1 for m in moved]
            if max(abs(s) for s in shift) <= 1:
                source = (moved[0] & 1) * 4 + (moved[1] & 1) * 2 + (moved[2] & 1)
                delta = (shift[0] + 1) * 9 + (shift[1] + 1) * 3 + shift[2] + 1
                table[c, number] = delta * 8 + source
    return table.reshape(-1)


def groups():
    runs = []
    for number, offset in enumerate(direction_table()):
        classes = tuple(
            c for c in range(8)
            if all(
                abs(offset[k]) < 3 or (c >> (2 - k) & 1) == (offset[k] < 0) for k in range(3)
            )
        )
        if runs and runs[-1][2] == classes:
            runs[-1][1] += 1
        else:
            runs.append([number, 1, classes])
    return runs


def grid_order(total_bits):
    order, extents = [], []
    for target in range(3):
        chosen = [k for k in range(total_bits - 1, -1, -1) if 2 - k % 3 == target]
        order += [total_bits - 1 - k for k in chosen]
        extents.append(2 ** len(chosen))
    return order, extents


def to_grid(rows, total_bits):
    order, extents = grid_order(total_bits)
    trailing = rows.shape[1:]
    bitwise = rows.reshape((2,) * total_bits + trailing)
    kept = tuple(range(total_bits, total_bits + len(trailing)))
    return jnp.transpose(bitwise, tuple(order) + kept).reshape(tuple(extents) + trailing)


def grid_index(morton, extents):
    coords = [0, 0, 0]
    for k in range(morton.bit_length()):
        coords[2 - k % 3] |= (morton >> k & 1) << (k // 3)
    return (coords[0] * extents[1] + coords[1]) * extents[2] + coords[2]


def halo_kernel(count, level_bits, fext, gext, fine, parent, out_f, out_p, ext_f, ext_p, sent, got):
    me = lax.axis_index("box")
    levels = ((fine, ext_f, fext), (parent, ext_p, gext))
    for _, ext, _ in levels:
        ext[...] = jnp.zeros_like(ext)
    for block, ext, (sx, sy, sz) in levels:
        for m in range(sx * sy * sz):
            at = grid_index(m, (sx, sy, sz))
            ext[1 + at // (sy * sz), 1 + at // sz % sy, 1 + at % sz] = block[m]

    around = []
    for dim in range(3):
        owned = [k for k in range(count.bit_length() - 1) if 2 - (level_bits + k) % 3 == dim]
        at = sum((me // 2**k % 2) * 2**n for n, k in enumerate(owned))
        base = me - sum((me // 2**k % 2) * 2**k for k in owned)
        sides = []
        for step in (1, -1):
            to = at + step + 2 ** len(owned)
            dst = base + sum((to // 2**n % 2) * 2**k for n, k in enumerate(owned))
            inside = at < 2 ** len(owned) - 1 if step == 1 else at > 0
            sides.append((inside, dst))
        around.append(sides)

    barrier = pltpu.get_barrier_semaphore()
    for sides in around:
        for inside, dst in sides:
            @pl.when(inside)
            def _(dst=dst):
                pl.semaphore_signal(
                    barrier, inc=1, device_id=(dst,), device_id_type=pl.DeviceIdType.MESH
                )
    peers = sum(inside.astype(jnp.int32) for sides in around for inside, _ in sides)
    pl.semaphore_wait(barrier, peers)

    for dim in range(3):
        copies = []
        for level, (_, ext, size) in enumerate(levels):
            for side in range(2):
                rest = [
                    pl.ds(0, size[k] + 2) if k < dim else pl.ds(1, size[k]) for k in range(3)
                ]
                src, dst = list(rest), list(rest)
                src[dim] = pl.ds(size[dim] if side == 0 else 1, 1)
                dst[dim] = pl.ds(0 if side == 0 else size[dim] + 1, 1)
                copy = pltpu.make_async_remote_copy(
                    src_ref=ext.at[tuple(src)],
                    dst_ref=ext.at[tuple(dst)],
                    send_sem=sent.at[dim, level, side],
                    recv_sem=got.at[dim, level, side],
                    device_id=(around[dim][side][1],),
                    device_id_type=pl.DeviceIdType.MESH,
                )
                copies.append((copy, around[dim][side][0], around[dim][1 - side][0]))
        for copy, to, source in copies:
            pl.when(to)(copy.start)
        for copy, to, source in copies:
            pl.when(source)(copy.wait_recv)
        for copy, to, source in copies:
            pl.when(to)(copy.wait_send)

    for ext, out, size in ((ext_f, out_f, fext), (ext_p, out_p, gext)):
        line = (size[2] + 2) * 8
        for x in range(size[0] + 2):
            for y in range(size[1] + 2):
                rows = ext[x, y].astype(jnp.float32).reshape(line, ext.shape[4])
                out[pl.ds((x * (size[1] + 2) + y) * line, line), :] = rows


def exchange(fine_mult, parent_mult, fbits, fext, gext):
    count, width = lax.axis_size("box"), fine_mult.shape[1]
    wide = [tuple(e + 2 for e in ext) for ext in (fext, gext)]
    vmem = pl.BlockSpec(memory_space=pltpu.VMEM)
    return pl.pallas_call(
        functools.partial(halo_kernel, count, fbits + 3, fext, gext),
        out_shape=[
            jax.ShapeDtypeStruct((w[0] * w[1] * w[2] * 8, width), jnp.float32) for w in wide
        ],
        in_specs=[vmem, vmem],
        out_specs=[vmem, vmem],
        scratch_shapes=[pltpu.VMEM(w + (8, width), jnp.bfloat16) for w in wide]
        + [pltpu.SemaphoreType.DMA((3, 2, 2)), pltpu.SemaphoreType.DMA((3, 2, 2))],
        compiler_params=pltpu.CompilerParams(
            collective_id=0, has_side_effects=True, vmem_limit_bytes=32 * 1024 * 1024
        ),
        name="halo",
    )(fine_mult.reshape(-1, 8, width), parent_mult.reshape(-1, 8, width))


def interact_kernel(
    fext, gext, wtab, ext_f, ext_p, words, bits, shift, kernels,
    fine_out, parent_out, kv, win, wb, acc, acc_f, acc_p, par, sem,
):
    nf, ng = fext[0] * fext[1] * fext[2], gext[0] * gext[1] * gext[2]
    rows = nf + ng
    tiles = rows // 16
    fetch = pltpu.make_async_copy(kernels, kv, sem)
    fetch.start()

    def build(index, carry):
        delta, source = index // 8, index % 8
        dx, dy, dz = delta // 9, delta // 3 % 3, delta % 3
        for ref, ext, base in ((ext_f, fext, 0), (ext_p, gext, nf)):
            got = []
            for x in range(ext[0]):
                for y in range(ext[1]):
                    first = ((x + dx) * (ext[1] + 2) + y + dy) * (ext[2] + 2) + dz
                    got.append(ref[pl.ds(first * 8 + source, ext[2], stride=8), :])
            stack = jnp.concatenate(got, axis=0).astype(jnp.bfloat16)
            count = stack.shape[0] // 16
            win[index, pl.ds(base // 16, count)] = stack.reshape(count, 16, 128)
        return carry

    lax.fori_loop(0, 216, build, 0)
    fetch.wait()

    def spread(c, carry):
        mine = words[c]
        for w in range(20):
            wide = jnp.broadcast_to(mine[:, w : w + 1], (rows, 128)).astype(jnp.int16)
            wb[c, w] = wide.reshape(tiles, 16, 128)
        acc[c] = jnp.zeros((rows, 128), jnp.float32)
        return carry

    lax.fori_loop(0, 8, spread, 0)

    def contract(start, count, classes):
        lhs = []
        for c in classes:
            line = []
            for i in range(count):
                d = start + i
                hit = (wb[c, d // 16] & bits[d % 16][None]) != 0
                x = win[wtab[c * 316 + d]]
                line.append(jnp.where(hit, x, jnp.zeros_like(x)).reshape(rows, 128))
            lhs.append(jnp.concatenate(line, axis=1))
        total = jnp.dot(
            jnp.concatenate(lhs, axis=0),
            kv[pl.ds(start, count)].reshape(count * 128, 128),
            preferred_element_type=jnp.float32,
        )
        for k, c in enumerate(classes):
            acc[c] += total[k * rows : (k + 1) * rows]

    for start, count, classes in groups():
        if count > CHUNK and len(classes) == 8:
            def step(j, carry, start=start, classes=classes):
                contract(start + j * CHUNK, CHUNK, classes)
                return carry

            lax.fori_loop(0, count // CHUNK, step, 0)
        else:
            contract(start, count, classes)

    for c in range(8):
        acc_f[pl.ds(c * nf, nf), :] = acc[c, :nf]
        acc_p[pl.ds(c * ng, ng), :] = (
            (acc[c, nf:] * 0.5).astype(jnp.bfloat16).astype(jnp.float32)
        )
    for c in range(8):
        cx, cy, cz = c >> 2 & 1, c >> 1 & 1, c & 1
        for gx in range(gext[0]):
            for gy in range(gext[1]):
                first = c * ng + (gx * gext[1] + gy) * gext[2]
                to = ((2 * gx + cx) * fext[1] + 2 * gy + cy) * fext[2] + cz
                par[pl.ds(to, gext[2], stride=2), :] = acc_p[pl.ds(first, gext[2]), :]
    local = par[...].astype(jnp.bfloat16)
    for c in range(8):
        acc_f[pl.ds(c * nf, nf), :] += jnp.dot(
            local, shift[c], preferred_element_type=jnp.float32
        )
    for ref, out, ext, total in ((acc_f, fine_out, fext, nf), (acc_p, parent_out, gext, ng)):
        for m in range(0, total, 2):
            pair = [
                ref[pl.ds(grid_index(m + k, ext), 8, stride=total), :] for k in range(2)
            ]
            out[pl.ds(m * 8, 16), :] = jnp.concatenate(pair, axis=0).astype(jnp.bfloat16)


def on_device(fine_mult, parent_mult, fine_mask, parent_mask, kernels, shift_ops):
    width = fine_mult.shape[1]
    fbits = fine_mult.shape[0].bit_length() - 4
    pbits = parent_mult.shape[0].bit_length() - 4
    fext, gext = tuple(grid_order(fbits)[1]), tuple(grid_order(pbits)[1])
    nf, ng = 2**fbits, 2**pbits
    rows = nf + ng

    ext_f, ext_p = exchange(fine_mult, parent_mult, fbits, fext, gext)

    def by_class(mask, bits, total):
        grid = to_grid(jnp.transpose(mask).reshape(total, 8, 20), bits)
        return jnp.transpose(grid.reshape(total, 8, 20), (1, 0, 2))

    words = jnp.concatenate(
        [by_class(fine_mask, fbits, nf), by_class(parent_mask, pbits, ng)], axis=1
    )
    wtab = window_table()
    flags = np.array([1 << k if k < 15 else -(1 << 15) for k in range(16)], np.int16)
    bits = np.broadcast_to(flags[:, None, None], (16, 16, 128))
    smem = pl.BlockSpec(memory_space=pltpu.SMEM)
    vmem = pl.BlockSpec(memory_space=pltpu.VMEM)
    return pl.pallas_call(
        functools.partial(interact_kernel, fext, gext),
        out_shape=[
            jax.ShapeDtypeStruct(fine_mult.shape, jnp.bfloat16),
            jax.ShapeDtypeStruct(parent_mult.shape, jnp.bfloat16),
        ],
        in_specs=[smem, vmem, vmem, vmem, vmem, vmem, pl.BlockSpec(memory_space=pl.ANY)],
        out_specs=[vmem, vmem],
        scratch_shapes=[
            pltpu.VMEM(kernels.shape, jnp.bfloat16),
            pltpu.VMEM((216, rows // 16, 16, width), jnp.bfloat16),
            pltpu.VMEM((8, 20, rows // 16, 16, width), jnp.int16),
            pltpu.VMEM((8, rows, width), jnp.float32),
            pltpu.VMEM((8 * nf, width), jnp.float32),
            pltpu.VMEM((8 * ng, width), jnp.float32),
            pltpu.VMEM((nf, width), jnp.float32),
            pltpu.SemaphoreType.DMA,
        ],
        compiler_params=pltpu.CompilerParams(vmem_limit_bytes=56 * 1024 * 1024),
        cost_estimate=pl.CostEstimate(
            flops=2 * 8 * rows * 189 * width * width,
            bytes_accessed=kernels.size * 2,
            transcendentals=0,
        ),
        name="interact",
    )(wtab, ext_f, ext_p, words, jnp.asarray(bits), shift_ops, kernels)


def solution(mesh):
    return jax.shard_map(
        on_device,
        mesh=mesh,
        in_specs=(P("box", None), P("box", None), P(None, "box"), P(None, "box"), P(), P()),
        out_specs=(P("box", None), P("box", None)),
        check_vma=False,
    )
```

```python
import functools

import jax
import jax.numpy as jnp
import numpy as np
from jax import lax
from jax.experimental import pallas as pl
from jax.experimental.pallas import tpu as pltpu
from jax.sharding import PartitionSpec as P

CHUNK = 14


def direction_table():
    listing = []
    for g1 in range(3):
        for g2 in range(3):
            for g3 in range(3):
                spans = [([-2, -1, 0, 1, 2], [-3], [3])[g] for g in (g1, g2, g3)]
                for o1 in spans[0]:
                    for o2 in spans[1]:
                        for o3 in spans[2]:
                            if max(abs(o1), abs(o2), abs(o3)) >= 2:
                                listing.append((o1, o2, o3))
    return listing


def window_table():
    table = np.zeros((8, 316), np.int32)
    for c in range(8):
        child = (c >> 2 & 1, c >> 1 & 1, c & 1)
        for number, offset in enumerate(direction_table()):
            moved = [child[k] + offset[k] for k in range(3)]
            shift = [m >> 1 for m in moved]
            if max(abs(s) for s in shift) <= 1:
                source = (moved[0] & 1) * 4 + (moved[1] & 1) * 2 + (moved[2] & 1)
                delta = (shift[0] + 1) * 9 + (shift[1] + 1) * 3 + shift[2] + 1
                table[c, number] = delta * 8 + source
    return table.reshape(-1)


def groups():
    runs = []
    for number, offset in enumerate(direction_table()):
        classes = tuple(
            c for c in range(8)
            if all(
                abs(offset[k]) < 3 or (c >> (2 - k) & 1) == (offset[k] < 0) for k in range(3)
            )
        )
        if runs and runs[-1][2] == classes:
            runs[-1][1] += 1
        else:
            runs.append([number, 1, classes])
    return runs


def grid_order(total_bits):
    order, extents = [], []
    for target in range(3):
        chosen = [k for k in range(total_bits - 1, -1, -1) if 2 - k % 3 == target]
        order += [total_bits - 1 - k for k in chosen]
        extents.append(2 ** len(chosen))
    return order, extents


def to_grid(rows, total_bits):
    order, extents = grid_order(total_bits)
    trailing = rows.shape[1:]
    bitwise = rows.reshape((2,) * total_bits + trailing)
    kept = tuple(range(total_bits, total_bits + len(trailing)))
    return jnp.transpose(bitwise, tuple(order) + kept).reshape(tuple(extents) + trailing)


def grid_index(morton, extents):
    coords = [0, 0, 0]
    for k in range(morton.bit_length()):
        coords[2 - k % 3] |= (morton >> k & 1) << (k // 3)
    return (coords[0] * extents[1] + coords[1]) * extents[2] + coords[2]


def halo_kernel(
    count, level_bits, fext, gext, fine, parent, fmask, pmask, out_f, out_p, wb,
    ext_f, ext_p, turned_f, turned_p, sent, got,
):
    me = lax.axis_index("box")
    levels = ((fine, ext_f, fext), (parent, ext_p, gext))
    for _, ext, _ in levels:
        ext[...] = jnp.zeros_like(ext)
    for block, ext, (sx, sy, sz) in levels:
        for m in range(sx * sy * sz):
            at = grid_index(m, (sx, sy, sz))
            ext[1 + at // (sy * sz), 1 + at // sz % sy, 1 + at % sz] = block[m]

    around = []
    for dim in range(3):
        owned = [k for k in range(count.bit_length() - 1) if 2 - (level_bits + k) % 3 == dim]
        at = sum((me // 2**k % 2) * 2**n for n, k in enumerate(owned))
        base = me - sum((me // 2**k % 2) * 2**k for k in owned)
        sides = []
        for step in (1, -1):
            to = at + step + 2 ** len(owned)
            dst = base + sum((to // 2**n % 2) * 2**k for n, k in enumerate(owned))
            inside = at < 2 ** len(owned) - 1 if step == 1 else at > 0
            sides.append((inside, dst))
        around.append(sides)

    barrier = pltpu.get_barrier_semaphore()
    for sides in around:
        for inside, dst in sides:
            @pl.when(inside)
            def _(dst=dst):
                pl.semaphore_signal(
                    barrier, inc=1, device_id=(dst,), device_id_type=pl.DeviceIdType.MESH
                )
    peers = sum(inside.astype(jnp.int32) for sides in around for inside, _ in sides)
    pl.semaphore_wait(barrier, peers)

    nf, ng = fext[0] * fext[1] * fext[2], gext[0] * gext[1] * gext[2]
    rows = nf + ng

    def turn(mask, turned, ext):
        boxes = mask.shape[1]
        for first in range(0, boxes, 128):
            block = jnp.concatenate(
                [mask[:16, first : first + 128], mask[16:, first : first + 128],
                 jnp.zeros((108, 128), jnp.int32)], axis=0,
            ).T
            for k in range(16):
                at = grid_index(first // 8 + k, ext)
                turned[pl.ds(at * 8, 8), :] = block[k * 8 : k * 8 + 8]

    def spread(c):
        mine = jnp.concatenate(
            [turned_f[pl.ds(c, nf, stride=8), :], turned_p[pl.ds(c, ng, stride=8), :]], axis=0
        )
        for w in range(20):
            wide = jnp.broadcast_to(mine[:, w : w + 1], (rows, 128)).astype(jnp.int16)
            wb[c, w] = wide.reshape(rows // 16, 16, 128)

    for dim in range(3):
        copies = []
        for level, (_, ext, size) in enumerate(levels):
            for side in range(2):
                rest = [
                    pl.ds(0, size[k] + 2) if k < dim else pl.ds(1, size[k]) for k in range(3)
                ]
                src, dst = list(rest), list(rest)
                src[dim] = pl.ds(size[dim] if side == 0 else 1, 1)
                dst[dim] = pl.ds(0 if side == 0 else size[dim] + 1, 1)
                copy = pltpu.make_async_remote_copy(
                    src_ref=ext.at[tuple(src)],
                    dst_ref=ext.at[tuple(dst)],
                    send_sem=sent.at[dim, level, side],
                    recv_sem=got.at[dim, level, side],
                    device_id=(around[dim][side][1],),
                    device_id_type=pl.DeviceIdType.MESH,
                )
                copies.append((copy, around[dim][side][0], around[dim][1 - side][0]))
        for copy, to, source in copies:
            pl.when(to)(copy.start)
        if dim == 0:
            turn(fmask, turned_f, fext)
            turn(pmask, turned_p, gext)
        for c in ((0, 1), (2, 3, 4), (5, 6, 7))[dim]:
            spread(c)
        for copy, to, source in copies:
            pl.when(source)(copy.wait_recv)
        for copy, to, source in copies:
            pl.when(to)(copy.wait_send)

    for ext, out, size in ((ext_f, out_f, fext), (ext_p, out_p, gext)):
        line = (size[2] + 2) * 8
        for x in range(size[0] + 2):
            for y in range(size[1] + 2):
                rows = ext[x, y].astype(jnp.float32).reshape(line, ext.shape[4])
                out[pl.ds((x * (size[1] + 2) + y) * line, line), :] = rows


def exchange(fine_mult, parent_mult, fine_mask, parent_mask, fbits, fext, gext):
    count, width = lax.axis_size("box"), fine_mult.shape[1]
    wide = [tuple(e + 2 for e in ext) for ext in (fext, gext)]
    boxes = [fine_mult.shape[0], parent_mult.shape[0]]
    vmem = pl.BlockSpec(memory_space=pltpu.VMEM)
    return pl.pallas_call(
        functools.partial(halo_kernel, count, fbits + 3, fext, gext),
        out_shape=[
            jax.ShapeDtypeStruct((w[0] * w[1] * w[2] * 8, width), jnp.float32) for w in wide
        ] + [jax.ShapeDtypeStruct((8, 20, sum(boxes) // 128, 16, width), jnp.int16)],
        in_specs=[vmem] * 4,
        out_specs=[vmem] * 3,
        scratch_shapes=[pltpu.VMEM(w + (8, width), jnp.bfloat16) for w in wide]
        + [pltpu.VMEM((b, 128), jnp.int32) for b in boxes]
        + [pltpu.SemaphoreType.DMA((3, 2, 2)), pltpu.SemaphoreType.DMA((3, 2, 2))],
        compiler_params=pltpu.CompilerParams(
            collective_id=0, has_side_effects=True, vmem_limit_bytes=24 * 1024 * 1024
        ),
        name="halo",
    )(
        fine_mult.reshape(-1, 8, width), parent_mult.reshape(-1, 8, width), fine_mask, parent_mask
    )


def interact_kernel(
    fext, gext, wtab, ext_f, ext_p, wb, shift_ops, kernels,
    fine_out, parent_out, kv, win, shift, bits, acc, acc_f, acc_p, par, sem,
):
    nf, ng = fext[0] * fext[1] * fext[2], gext[0] * gext[1] * gext[2]
    rows = nf + ng
    tiles = rows // 16
    fetch = pltpu.make_async_copy(kernels, kv, sem.at[0])
    fetch.start()
    fetch_shift = pltpu.make_async_copy(shift_ops, shift, sem.at[1])
    fetch_shift.start()
    for k in range(16):
        bits[k] = jnp.full((16, 128), 1 << k if k < 15 else -(1 << 15), jnp.int16)
    acc[...] = jnp.zeros_like(acc)

    def build(delta, carry):
        dx, dy, dz = delta // 9, delta // 3 % 3, delta % 3
        for ref, ext, base in ((ext_f, fext, 0), (ext_p, gext, nf)):
            for source in range(8):
                got = []
                for x in range(ext[0]):
                    for y in range(ext[1]):
                        first = ((x + dx) * (ext[1] + 2) + y + dy) * (ext[2] + 2) + dz
                        got.append(ref[pl.ds(first * 8 + source, ext[2], stride=8), :])
                stack = jnp.concatenate(got, axis=0).astype(jnp.bfloat16)
                count = stack.shape[0] // 16
                win[delta * 8 + source, pl.ds(base // 16, count)] = stack.reshape(count, 16, 128)
        return carry

    lax.fori_loop(0, 27, build, 0)
    fetch.wait()

    def contract(start, count, classes):
        lhs = []
        for c in classes:
            line = []
            for i in range(count):
                d = start + i
                hit = (wb[c, d // 16] & bits[d % 16][None]) != 0
                x = win[wtab[c * 316 + d]]
                line.append(jnp.where(hit, x, jnp.zeros_like(x)).reshape(rows, 128))
            lhs.append(jnp.concatenate(line, axis=1))
        total = jnp.dot(
            jnp.concatenate(lhs, axis=0),
            kv[pl.ds(start, count)].reshape(count * 128, 128),
            preferred_element_type=jnp.float32,
        )
        for k, c in enumerate(classes):
            acc[c] += total[k * rows : (k + 1) * rows]

    for start, count, classes in groups():
        if count > CHUNK and len(classes) == 8:
            def step(j, carry, start=start, classes=classes):
                contract(start + j * CHUNK, CHUNK, classes)
                return carry

            lax.fori_loop(0, count // CHUNK, step, 0)
        else:
            contract(start, count, classes)

    for c in range(8):
        acc_f[pl.ds(c * nf, nf), :] = acc[c, :nf]
        acc_p[pl.ds(c * ng, ng), :] = (
            (acc[c, nf:] * 0.5).astype(jnp.bfloat16).astype(jnp.float32)
        )
    for c in range(8):
        cx, cy, cz = c >> 2 & 1, c >> 1 & 1, c & 1
        for gx in range(gext[0]):
            for gy in range(gext[1]):
                first = c * ng + (gx * gext[1] + gy) * gext[2]
                to = ((2 * gx + cx) * fext[1] + 2 * gy + cy) * fext[2] + cz
                par[pl.ds(to, gext[2], stride=2), :] = acc_p[pl.ds(first, gext[2]), :]
    local = par[...].astype(jnp.bfloat16)
    fetch_shift.wait()
    for c in range(8):
        acc_f[pl.ds(c * nf, nf), :] += jnp.dot(
            local, shift[c], preferred_element_type=jnp.float32
        )
    for ref, out, ext, total in ((acc_f, fine_out, fext, nf), (acc_p, parent_out, gext, ng)):
        for m in range(0, total, 2):
            pair = [
                ref[pl.ds(grid_index(m + k, ext), 8, stride=total), :] for k in range(2)
            ]
            out[pl.ds(m * 8, 16), :] = jnp.concatenate(pair, axis=0).astype(jnp.bfloat16)


def on_device(fine_mult, parent_mult, fine_mask, parent_mask, kernels, shift_ops):
    width = fine_mult.shape[1]
    fbits = fine_mult.shape[0].bit_length() - 4
    pbits = parent_mult.shape[0].bit_length() - 4
    fext, gext = tuple(grid_order(fbits)[1]), tuple(grid_order(pbits)[1])
    nf, ng = 2**fbits, 2**pbits
    rows = nf + ng

    ext_f, ext_p, wb = exchange(
        fine_mult, parent_mult, fine_mask, parent_mask, fbits, fext, gext
    )
    wtab = window_table()
    smem = pl.BlockSpec(memory_space=pltpu.SMEM)
    hbm = pl.BlockSpec(memory_space=pl.ANY)
    vmem = pl.BlockSpec(memory_space=pltpu.VMEM)
    return pl.pallas_call(
        functools.partial(interact_kernel, fext, gext),
        out_shape=[
            jax.ShapeDtypeStruct(fine_mult.shape, jnp.bfloat16),
            jax.ShapeDtypeStruct(parent_mult.shape, jnp.bfloat16),
        ],
        in_specs=[smem, vmem, vmem, vmem, hbm, hbm],
        out_specs=[vmem, vmem],
        scratch_shapes=[
            pltpu.VMEM(kernels.shape, jnp.bfloat16),
            pltpu.VMEM((216, rows // 16, 16, width), jnp.bfloat16),
            pltpu.VMEM(shift_ops.shape, jnp.bfloat16),
            pltpu.VMEM((16, 16, width), jnp.int16),
            pltpu.VMEM((8, rows, width), jnp.float32),
            pltpu.VMEM((8 * nf, width), jnp.float32),
            pltpu.VMEM((8 * ng, width), jnp.float32),
            pltpu.VMEM((nf, width), jnp.float32),
            pltpu.SemaphoreType.DMA((2,)),
        ],
        compiler_params=pltpu.CompilerParams(vmem_limit_bytes=44 * 1024 * 1024),
        cost_estimate=pl.CostEstimate(
            flops=2 * 8 * rows * 189 * width * width,
            bytes_accessed=kernels.size * 2,
            transcendentals=0,
        ),
        name="interact",
    )(wtab, ext_f, ext_p, wb, shift_ops, kernels)


def solution(mesh):
    return jax.shard_map(
        on_device,
        mesh=mesh,
        in_specs=(P("box", None), P("box", None), P(None, "box"), P(None, "box"), P(), P()),
        out_specs=(P("box", None), P("box", None)),
        check_vma=False,
    )
```

```python
import functools

import jax
import jax.numpy as jnp
import numpy as np
from jax import lax
from jax.experimental import pallas as pl
from jax.experimental.pallas import tpu as pltpu
from jax.sharding import PartitionSpec as P

CHUNK = 14


def direction_table():
    listing = []
    for g1 in range(3):
        for g2 in range(3):
            for g3 in range(3):
                spans = [([-2, -1, 0, 1, 2], [-3], [3])[g] for g in (g1, g2, g3)]
                for o1 in spans[0]:
                    for o2 in spans[1]:
                        for o3 in spans[2]:
                            if max(abs(o1), abs(o2), abs(o3)) >= 2:
                                listing.append((o1, o2, o3))
    return listing


def window_table():
    table = np.zeros((8, 316), np.int32)
    for c in range(8):
        child = (c >> 2 & 1, c >> 1 & 1, c & 1)
        for number, offset in enumerate(direction_table()):
            moved = [child[k] + offset[k] for k in range(3)]
            shift = [m >> 1 for m in moved]
            if max(abs(s) for s in shift) <= 1:
                source = (moved[0] & 1) * 4 + (moved[1] & 1) * 2 + (moved[2] & 1)
                delta = (shift[0] + 1) * 9 + (shift[1] + 1) * 3 + shift[2] + 1
                table[c, number] = delta * 8 + source
    return table.reshape(-1)


def groups():
    runs = []
    for number, offset in enumerate(direction_table()):
        classes = tuple(
            c for c in range(8)
            if all(
                abs(offset[k]) < 3 or (c >> (2 - k) & 1) == (offset[k] < 0) for k in range(3)
            )
        )
        if runs and runs[-1][2] == classes:
            runs[-1][1] += 1
        else:
            runs.append([number, 1, classes])
    return runs


def grid_order(total_bits):
    order, extents = [], []
    for target in range(3):
        chosen = [k for k in range(total_bits - 1, -1, -1) if 2 - k % 3 == target]
        order += [total_bits - 1 - k for k in chosen]
        extents.append(2 ** len(chosen))
    return order, extents


def to_grid(rows, total_bits):
    order, extents = grid_order(total_bits)
    trailing = rows.shape[1:]
    bitwise = rows.reshape((2,) * total_bits + trailing)
    kept = tuple(range(total_bits, total_bits + len(trailing)))
    return jnp.transpose(bitwise, tuple(order) + kept).reshape(tuple(extents) + trailing)


def grid_index(morton, extents):
    coords = [0, 0, 0]
    for k in range(morton.bit_length()):
        coords[2 - k % 3] |= (morton >> k & 1) << (k // 3)
    return (coords[0] * extents[1] + coords[1]) * extents[2] + coords[2]


def halo_kernel(
    count, level_bits, fext, gext, fine_in, parent_in, fmask_in, pmask_in, out_f, out_p, wb,
    ext_f, ext_p, turned_f, turned_p, fine, parent, fmask, pmask, sent, got, fetched,
):
    fetches = [
        pltpu.make_async_copy(src, dst, fetched.at[k])
        for k, (src, dst) in enumerate(
            ((fine_in, fine), (parent_in, parent), (fmask_in, fmask), (pmask_in, pmask))
        )
    ]
    for fetch in fetches:
        fetch.start()
    me = lax.axis_index("box")
    levels = ((fine, ext_f, fext), (parent, ext_p, gext))
    for _, ext, _ in levels:
        ext[...] = jnp.zeros_like(ext)
    around = []
    for dim in range(3):
        owned = [k for k in range(count.bit_length() - 1) if 2 - (level_bits + k) % 3 == dim]
        at = sum((me // 2**k % 2) * 2**n for n, k in enumerate(owned))
        base = me - sum((me // 2**k % 2) * 2**k for k in owned)
        sides = []
        for step in (1, -1):
            to = at + step + 2 ** len(owned)
            dst = base + sum((to // 2**n % 2) * 2**k for n, k in enumerate(owned))
            inside = at < 2 ** len(owned) - 1 if step == 1 else at > 0
            sides.append((inside, dst))
        around.append(sides)

    barrier = pltpu.get_barrier_semaphore()
    for sides in around:
        for inside, dst in sides:
            @pl.when(inside)
            def _(dst=dst):
                pl.semaphore_signal(
                    barrier, inc=1, device_id=(dst,), device_id_type=pl.DeviceIdType.MESH
                )
    for fetch in fetches:
        fetch.wait()
    for block, ext, (sx, sy, sz) in levels:
        for m in range(sx * sy * sz):
            at = grid_index(m, (sx, sy, sz))
            ext[1 + at // (sy * sz), 1 + at // sz % sy, 1 + at % sz] = block[m]

    peers = sum(inside.astype(jnp.int32) for sides in around for inside, _ in sides)
    pl.semaphore_wait(barrier, peers)

    nf, ng = fext[0] * fext[1] * fext[2], gext[0] * gext[1] * gext[2]
    rows = nf + ng

    def turn(mask, turned, ext):
        boxes = mask.shape[1]
        for first in range(0, boxes, 128):
            block = jnp.concatenate(
                [mask[:16, first : first + 128], mask[16:, first : first + 128],
                 jnp.zeros((108, 128), jnp.int32)], axis=0,
            ).T
            for k in range(16):
                at = grid_index(first // 8 + k, ext)
                turned[pl.ds(at * 8, 8), :] = block[k * 8 : k * 8 + 8]

    def spread(c):
        mine = jnp.concatenate(
            [turned_f[pl.ds(c, nf, stride=8), :], turned_p[pl.ds(c, ng, stride=8), :]], axis=0
        )
        for w in range(20):
            wide = jnp.broadcast_to(mine[:, w : w + 1], (rows, 128)).astype(jnp.int16)
            wb[c, w] = wide.reshape(rows // 16, 16, 128)

    for dim in range(3):
        copies = []
        for level, (_, ext, size) in enumerate(levels):
            for side in range(2):
                rest = [
                    pl.ds(0, size[k] + 2) if k < dim else pl.ds(1, size[k]) for k in range(3)
                ]
                src, dst = list(rest), list(rest)
                src[dim] = pl.ds(size[dim] if side == 0 else 1, 1)
                dst[dim] = pl.ds(0 if side == 0 else size[dim] + 1, 1)
                copy = pltpu.make_async_remote_copy(
                    src_ref=ext.at[tuple(src)],
                    dst_ref=ext.at[tuple(dst)],
                    send_sem=sent.at[dim, level, side],
                    recv_sem=got.at[dim, level, side],
                    device_id=(around[dim][side][1],),
                    device_id_type=pl.DeviceIdType.MESH,
                )
                copies.append((copy, around[dim][side][0], around[dim][1 - side][0]))
        for copy, to, source in copies:
            pl.when(to)(copy.start)
        if dim == 0:
            turn(fmask, turned_f, fext)
            turn(pmask, turned_p, gext)
        for c in ((0, 1), (2, 3, 4), (5, 6, 7))[dim]:
            spread(c)
        for copy, to, source in copies:
            pl.when(source)(copy.wait_recv)
        for copy, to, source in copies:
            pl.when(to)(copy.wait_send)

    for ext, out, size in ((ext_f, out_f, fext), (ext_p, out_p, gext)):
        line = (size[2] + 2) * 8
        for x in range(size[0] + 2):
            for y in range(size[1] + 2):
                rows = ext[x, y].astype(jnp.float32).reshape(line, ext.shape[4])
                out[pl.ds((x * (size[1] + 2) + y) * line, line), :] = rows


def exchange(fine_mult, parent_mult, fine_mask, parent_mask, fbits, fext, gext):
    count, width = lax.axis_size("box"), fine_mult.shape[1]
    wide = [tuple(e + 2 for e in ext) for ext in (fext, gext)]
    boxes = [fine_mult.shape[0], parent_mult.shape[0]]
    vmem = pl.BlockSpec(memory_space=pltpu.VMEM)
    return pl.pallas_call(
        functools.partial(halo_kernel, count, fbits + 3, fext, gext),
        out_shape=[
            jax.ShapeDtypeStruct((w[0] * w[1] * w[2] * 8, width), jnp.float32) for w in wide
        ] + [jax.ShapeDtypeStruct((8, 20, sum(boxes) // 128, 16, width), jnp.int16)],
        in_specs=[pl.BlockSpec(memory_space=pltpu.HBM)] * 4,
        out_specs=[vmem] * 3,
        scratch_shapes=[pltpu.VMEM(w + (8, width), jnp.bfloat16) for w in wide]
        + [pltpu.VMEM((b, 128), jnp.int32) for b in boxes]
        + [
            pltpu.VMEM((boxes[0] // 8, 8, width), jnp.bfloat16),
            pltpu.VMEM((boxes[1] // 8, 8, width), jnp.bfloat16),
            pltpu.VMEM(fine_mask.shape, jnp.int32),
            pltpu.VMEM(parent_mask.shape, jnp.int32),
            pltpu.SemaphoreType.DMA((3, 2, 2)),
            pltpu.SemaphoreType.DMA((3, 2, 2)),
            pltpu.SemaphoreType.DMA((4,)),
        ],
        compiler_params=pltpu.CompilerParams(
            collective_id=0, has_side_effects=True, vmem_limit_bytes=54 * 1024 * 1024
        ),
        name="halo",
    )(
        fine_mult.reshape(-1, 8, width), parent_mult.reshape(-1, 8, width), fine_mask, parent_mask
    )


def interact_kernel(
    fext, gext, wtab, ext_f, ext_p, wb, shift_ops, kernels,
    fine_out, parent_out, kv, win, shift, bits, acc, acc_f, acc_p, par, sem,
):
    nf, ng = fext[0] * fext[1] * fext[2], gext[0] * gext[1] * gext[2]
    rows = nf + ng
    tiles = rows // 16
    fetch = pltpu.make_async_copy(kernels, kv, sem.at[0])
    fetch.start()
    fetch_shift = pltpu.make_async_copy(shift_ops, shift, sem.at[1])
    fetch_shift.start()
    for k in range(16):
        bits[k] = jnp.full((16, 128), 1 << k if k < 15 else -(1 << 15), jnp.int16)
    acc[...] = jnp.zeros_like(acc)

    def build(delta, carry):
        dx, dy, dz = delta // 9, delta // 3 % 3, delta % 3
        for ref, ext, base in ((ext_f, fext, 0), (ext_p, gext, nf)):
            for source in range(8):
                got = []
                for x in range(ext[0]):
                    for y in range(ext[1]):
                        first = ((x + dx) * (ext[1] + 2) + y + dy) * (ext[2] + 2) + dz
                        got.append(ref[pl.ds(first * 8 + source, ext[2], stride=8), :])
                stack = jnp.concatenate(got, axis=0).astype(jnp.bfloat16)
                count = stack.shape[0] // 16
                win[delta * 8 + source, pl.ds(base // 16, count)] = stack.reshape(count, 16, 128)
        return carry

    lax.fori_loop(0, 27, build, 0)
    fetch.wait()

    def contract(start, count, classes):
        lhs = []
        for c in classes:
            line = []
            for i in range(count):
                d = start + i
                hit = (wb[c, d // 16] & bits[d % 16][None]) != 0
                x = win[wtab[c * 316 + d]]
                line.append(jnp.where(hit, x, jnp.zeros_like(x)).reshape(rows, 128))
            lhs.append(jnp.concatenate(line, axis=1))
        total = jnp.dot(
            jnp.concatenate(lhs, axis=0),
            kv[pl.ds(start, count)].reshape(count * 128, 128),
            preferred_element_type=jnp.float32,
        )
        for k, c in enumerate(classes):
            acc[c] += total[k * rows : (k + 1) * rows]

    for start, count, classes in groups():
        if count > CHUNK and len(classes) == 8:
            def step(j, carry, start=start, classes=classes):
                contract(start + j * CHUNK, CHUNK, classes)
                return carry

            lax.fori_loop(0, count // CHUNK, step, 0)
        else:
            contract(start, count, classes)

    for c in range(8):
        acc_f[pl.ds(c * nf, nf), :] = acc[c, :nf]
        acc_p[pl.ds(c * ng, ng), :] = (
            (acc[c, nf:] * 0.5).astype(jnp.bfloat16).astype(jnp.float32)
        )
    for c in range(8):
        cx, cy, cz = c >> 2 & 1, c >> 1 & 1, c & 1
        for gx in range(gext[0]):
            for gy in range(gext[1]):
                first = c * ng + (gx * gext[1] + gy) * gext[2]
                to = ((2 * gx + cx) * fext[1] + 2 * gy + cy) * fext[2] + cz
                par[pl.ds(to, gext[2], stride=2), :] = acc_p[pl.ds(first, gext[2]), :]
    local = par[...].astype(jnp.bfloat16)
    fetch_shift.wait()
    for c in range(8):
        acc_f[pl.ds(c * nf, nf), :] += jnp.dot(
            local, shift[c], preferred_element_type=jnp.float32
        )
    for ref, out, ext, total in ((acc_f, fine_out, fext, nf), (acc_p, parent_out, gext, ng)):
        for m in range(0, total, 2):
            pair = [
                ref[pl.ds(grid_index(m + k, ext), 8, stride=total), :] for k in range(2)
            ]
            out[pl.ds(m * 8, 16), :] = jnp.concatenate(pair, axis=0).astype(jnp.bfloat16)


def on_device(fine_mult, parent_mult, fine_mask, parent_mask, kernels, shift_ops):
    width = fine_mult.shape[1]
    fbits = fine_mult.shape[0].bit_length() - 4
    pbits = parent_mult.shape[0].bit_length() - 4
    fext, gext = tuple(grid_order(fbits)[1]), tuple(grid_order(pbits)[1])
    nf, ng = 2**fbits, 2**pbits
    rows = nf + ng

    ext_f, ext_p, wb = exchange(
        fine_mult, parent_mult, fine_mask, parent_mask, fbits, fext, gext
    )
    wtab = window_table()
    smem = pl.BlockSpec(memory_space=pltpu.SMEM)
    hbm = pl.BlockSpec(memory_space=pltpu.HBM)
    vmem = pl.BlockSpec(memory_space=pltpu.VMEM)
    return pl.pallas_call(
        functools.partial(interact_kernel, fext, gext),
        out_shape=[
            jax.ShapeDtypeStruct(fine_mult.shape, jnp.bfloat16),
            jax.ShapeDtypeStruct(parent_mult.shape, jnp.bfloat16),
        ],
        in_specs=[smem, vmem, vmem, vmem, hbm, hbm],
        out_specs=[vmem, vmem],
        scratch_shapes=[
            pltpu.VMEM(kernels.shape, jnp.bfloat16),
            pltpu.VMEM((216, rows // 16, 16, width), jnp.bfloat16),
            pltpu.VMEM(shift_ops.shape, jnp.bfloat16),
            pltpu.VMEM((16, 16, width), jnp.int16),
            pltpu.VMEM((8, rows, width), jnp.float32),
            pltpu.VMEM((8 * nf, width), jnp.float32),
            pltpu.VMEM((8 * ng, width), jnp.float32),
            pltpu.VMEM((nf, width), jnp.float32),
            pltpu.SemaphoreType.DMA((2,)),
        ],
        compiler_params=pltpu.CompilerParams(vmem_limit_bytes=54 * 1024 * 1024),
        cost_estimate=pl.CostEstimate(
            flops=2 * 8 * rows * 189 * width * width,
            bytes_accessed=kernels.size * 2,
            transcendentals=0,
        ),
        name="interact",
    )(wtab, ext_f, ext_p, wb, shift_ops, kernels)


def solution(mesh):
    return jax.shard_map(
        on_device,
        mesh=mesh,
        in_specs=(P("box", None), P("box", None), P(None, "box"), P(None, "box"), P(), P()),
        out_specs=(P("box", None), P("box", None)),
        check_vma=False,
    )
```
